32 devices in a mesh: gx: 4 (over z), gy: 8 (over y, x, core).
Axes of the slice: x: 2, y: 2, z: 4, core: 2. Of those that a mesh axis runs over, the one named last changes fastest.
Arguments:
- rhs: float32 [4, 128, 256, 128], P(None, 'gx', 'gy'), may hold values from -4.5 to 4.5
- coefficient: float32 [4, 128, 256, 128], P(None, 'gx', 'gy'), may hold values from 0.01 to 0.3
Outputs:
- solution: float32 [4, 128, 256, 128], P(None, 'gx', 'gy')
The draws below stay inside these ranges and needn't reach their ends.
All inputs are finite; a program needn't handle non-finite values.
Results may differ from the reference program's by a relative error of at most 0.0001.
Values sent between devices are 32-bit elements; how exact they have to be, the bound alone decides.
A program may use at most 320 MiB of HBM per device.

```python
import math
import jax
import jax.numpy as jnp
from jax import lax

NZ = 128
LEVELS = 6
SWEEPS = 2
NX = 128
NY = 256


def draw_rhs(key, part):
    key = jax.random.fold_in(key, 7)
    shape = (4, NX, NY, NZ)
    return jnp.clip(jax.random.normal(key, shape, jnp.float32), -4.5, 4.5)


def levels(key, dims, cuts, smallest, largest):
    def one(dim, blocks):
        draws = jax.random.uniform(jax.random.fold_in(jax.random.fold_in(key, 6), dim), (blocks,), jnp.float32, smallest / len(cuts), largest / len(cuts))
        return jnp.repeat(jnp.exp(draws), dims[dim] // blocks).reshape((-1,) + (1,) * (len(dims) - dim - 1))

    loudness = one(*cuts[0])
    for cut in cuts[1:]:
        loudness = loudness * one(*cut)
    return loudness


def setup_inputs(seed: int = 0) -> dict:
    key_list = jax.random.split(jax.random.key(seed), 3)
    rhs = draw_rhs(jax.random.fold_in(key_list[2], 71), 0)
    coefficient = jnp.clip(jnp.exp(math.log(0.3) - 3.4011974 * jax.random.uniform(key_list[1], (4, NX, NY, NZ), jnp.float32) ** levels(key_list[1], (4, NX, NY, NZ), ((1, 4), (2, 8)), -0.2, 0.2)), 0.01, 0.3)
    return {"rhs": rhs, "coefficient": coefficient}


def restrict(field):
    k, a, b, c = field.shape
    blocks = field.reshape(k, a // 2, 2, b // 2, 2, c // 2, 2)
    return blocks.sum(axis=(2, 4, 6)) * 0.125


def prolong(field):
    return jnp.repeat(jnp.repeat(jnp.repeat(field, 2, axis=1), 2, axis=2), 2, axis=3)


def neighbours(field):
    total = jnp.roll(field, -1, 1) + jnp.roll(field, 1, 1)
    total = total + jnp.roll(field, -1, 2) + jnp.roll(field, 1, 2)
    total = total + jnp.roll(field, -1, 3) + jnp.roll(field, 1, 3)
    return total


def parity_mask(shape):
    full = (1, shape[1], shape[2], shape[3])
    ix = lax.broadcasted_iota(jnp.int32, full, 1)
    iy = lax.broadcasted_iota(jnp.int32, full, 2)
    iz = lax.broadcasted_iota(jnp.int32, full, 3)
    return (ix + iy + iz) % 2


def sweeps(field, source, coef, scale, parity):
    denom = coef + 6.0 * scale
    for sweep in range(SWEEPS):
        for colour in (0, 1):
            fresh = (source + scale * neighbours(field)) / denom
            field = jnp.where(parity == colour, fresh, field)
    return field


def cycle(level, source, coefs):
    coef = coefs[level]
    scale = 0.25 ** level
    parity = parity_mask(source.shape)
    field = sweeps(jnp.zeros_like(source), source, coef, scale, parity)
    if level == LEVELS - 1:
        return field
    resid = source - (coef * field + scale * (6.0 * field - neighbours(field)))
    correction = cycle(level + 1, restrict(resid), coefs)
    field = field + prolong(correction)
    return sweeps(field, source, coef, scale, parity)


def reference(rhs, coefficient):
    coefs = [coefficient]
    for level in range(LEVELS - 1):
        coefs.append(restrict(coefs[-1]))
    return cycle(0, rhs, coefs)
```

```python
import functools
import jax
import jax.numpy as jnp
import numpy as np
from jax import lax
from jax.experimental import pallas as pl
from jax.experimental.pallas import tpu as pltpu
from jax.sharding import PartitionSpec as P

LEVELS = 6
SPLIT = 3
W = 4
L = 128
VMEM = pl.BlockSpec(memory_space=pltpu.VMEM)


def iota(shape, dim):
    return lax.broadcasted_iota(jnp.int32, shape, dim)


def z_sum(v, group):
    axis = v.ndim - 1
    if group == L:
        return pltpu.roll(v, 1, axis) + pltpu.roll(v, L - 1, axis)
    place = iota(v.shape, axis) % group
    up = jnp.where(place == group - 1, pltpu.roll(v, group - 1, axis), pltpu.roll(v, L - 1, axis))
    down = jnp.where(place == 0, pltpu.roll(v, L - group + 1, axis), pltpu.roll(v, 1, axis))
    return up + down


def y_sum(v):
    axis, n = v.ndim - 2, v.shape[-2]
    return pltpu.roll(v, 1, axis) + pltpu.roll(v, n - 1, axis)


def squeeze_matrix(half, scale):
    source, target = iota((L, L), 0), iota((L, L), 1)
    return jnp.where(target == source // 2 + half * (L // 2), scale, 0.0).astype(jnp.float32)


def spread_matrix(half):
    source, target = iota((L, L), 0), iota((L, L), 1)
    return jnp.where(source == target // 2 + half * (L // 2), 1.0, 0.0).astype(jnp.float32)


def dot(a, b):
    return jnp.dot(a, b, preferred_element_type=jnp.float32, precision=lax.Precision.HIGHEST)


def fold(part, first, rows):
    count, nx = part.shape[0], part.shape[1]
    outs = []
    for a in range(0, count, 2):
        total = None
        for h in range(min(2, count - a)):
            m = squeeze_matrix(h, 0.125)
            even = jnp.concatenate([part[a + h, x, pl.ds(first, rows, stride=2), :] for x in range(nx)], 0)
            odd = jnp.concatenate([part[a + h, x, pl.ds(first + 1, rows, stride=2), :] for x in range(nx)], 0)
            term = dot(even + odd, m)
            total = term if total is None else total + term
        outs.append(total.reshape(nx, rows, L))
    return outs


def half_sweep(v, f_ref, w_ref, colour, low, high, group):
    count, rows = v.shape[0], v.shape[2]
    parity = (iota((rows, L), 0) + iota((rows, L), 1)) % 2

    def body(step, carry):
        for k in range(2):
            x = low + 2 * step + k
            mask = parity == (colour + low + k) % 2
            for c in range(count):
                mid = v[c, x]
                total = v[c, x - 1] + v[c, x + 1] + y_sum(mid) + z_sum(mid, group)
                v[c, x] = jnp.where(mask, f_ref[c, x] + w_ref[c, x] * total, mid)
        return carry

    lax.fori_loop(0, (high - low) // 2, body, 0)


def down_kernel(scale, group, f_in, c_in, f_out, w_out, v_out, g_out, v, part):
    count, nx, ny = v_out.shape[0], v_out.shape[1], v_out.shape[2]
    ex = f_in.shape[1]
    rows = f_in.shape[2]
    parity = (iota((rows, L), 0) + iota((rows, L), 1)) % 2

    def first(step, carry):
        for k in range(2):
            x = 2 * step + k
            for c in range(count):
                inverse = 1.0 / (c_in[c, x] + 6.0 * scale)
                fd = f_in[c, x] * inverse
                f_out[c, x] = fd
                w_out[c, x] = scale * inverse
                v[c, x] = jnp.where(parity == k, fd, 0.0)
        return carry

    lax.fori_loop(0, ex // 2, first, 0)
    half_sweep(v, f_out, w_out, 1, 1, ex - 1, group)
    half_sweep(v, f_out, w_out, 0, 2, ex - 2, group)
    half_sweep(v, f_out, w_out, 1, 3, ex - 3, group)

    def last(step, carry):
        for c in range(count):
            total = None
            for k in range(2):
                x = W + 2 * step + k
                mid = v[c, x]
                nb = v[c, x - 1] + v[c, x + 1] + y_sum(mid) + z_sum(mid, group)
                r = f_in[c, x] - (c_in[c, x] * mid + scale * (6.0 * mid - nb))
                v_out[c, 2 * step + k] = v[c, x, W : W + ny, :]
                total = r if total is None else total + r
            part[c, step] = total
        return carry

    lax.fori_loop(0, nx // 2, last, 0)
    for a, g in enumerate(fold(part, W, ny // 2)):
        g_out[a] = g


def spread(e, half, t):
    q = dot(e, spread_matrix(half))
    n = q.shape[0]
    t[pl.ds(0, n, stride=2), :] = q
    t[pl.ds(1, n, stride=2), :] = q


def post(v, f_ref, w_ref, group):
    ex = v.shape[1]
    for p, colour in ((1, 0), (2, 1), (3, 0), (4, 1)):
        half_sweep(v, f_ref, w_ref, colour, p, ex - p, group)


def up_kernel(scale, group, t_in, f_in, w_in, *rest):
    if len(rest) == 2:
        out, v = rest
        fine = None
    else:
        fine, out, v, t = rest
    ex = t_in.shape[1]

    def copy(x, carry):
        for c in range(t_in.shape[0]):
            v[c, x] = t_in[c, x]
        return carry

    lax.fori_loop(0, ex, copy, 0)
    finish(v, f_in, w_in, group, fine, out, None if fine is None else t)


def finish(v, f_in, w_in, group, fine, out, t):
    post(v, f_in, w_in, group)
    ex, ey = v.shape[1], v.shape[2]
    nx, ny = ex - 2 * W, ey - 2 * W
    if fine is None:

        def give(x, carry):
            for c in range(v.shape[0]):
                out[c, x] = v[c, W + x, W : W + ny, :]
            return carry

        lax.fori_loop(0, nx, give, 0)
        return
    for c in range(v.shape[0]):
        for h in range(2):
            q = dot(v[c, W : W + nx, W : W + ny, :].reshape(nx * ny, L), spread_matrix(h)).reshape(nx, ny, L)
            for x in range(nx):
                t[x, pl.ds(0, ny, stride=2), :] = q[x]
                t[x, pl.ds(1, ny, stride=2), :] = q[x]
            for x in range(nx):
                for k in range(2):
                    out[2 * c + h, 2 * x + k] = fine[2 * c + h, 2 * x + k] + t[x]


def up_last_kernel(scale, group, t_in, e_in, f_in, w_in, fine, out, v, te, t):
    for i in range(e_in.shape[0]):
        q = dot(e_in[i], spread_matrix(0))
        n = q.shape[0]
        te[i, pl.ds(0, n, stride=2), :] = q
        te[i, pl.ds(1, n, stride=2), :] = q
        for k in range(2):
            v[0, 2 * i + k] = t_in[0, 2 * i + k] + te[i]
    finish(v, f_in, w_in, group, fine, out, t)


def whole_neighbours(v, group):
    up = jnp.concatenate([v[1:], v[:1]], 0)
    down = jnp.concatenate([v[-1:], v[:-1]], 0)
    return up + down + y_sum(v) + z_sum(v, group)


def whole_cycle(level, f, coef, group, scratch):
    scale = 0.25**level
    inverse = 1.0 / (coef + 6.0 * scale)
    fd, w = f * inverse, scale * inverse
    parity = (iota(f.shape, 0) + iota(f.shape, 1) + iota(f.shape, 2)) % 2

    def sweep(v, colour):
        return jnp.where(parity == colour, fd + w * whole_neighbours(v, group), v)

    v = jnp.where(parity == 0, fd, 0.0)
    v = sweep(sweep(sweep(v, 1), 0), 1)
    if level == LEVELS - 1:
        return v
    part = scratch[0]
    nx, ny = f.shape[0], f.shape[1]

    def coarse(u):
        pairs = u.reshape(nx // 2, 2, ny, L)
        part[0] = pairs[:, 0] + pairs[:, 1]
        return fold(part, 0, ny // 2)[0]

    g = coarse(f - (coef * v + scale * (6.0 * v - whole_neighbours(v, group))))
    c = coarse(coef)
    e = whole_cycle(level + 1, g, c, group // 2, scratch[1:])
    q = dot(e.reshape(nx // 2 * (ny // 2), L), spread_matrix(0)).reshape(nx // 2, ny // 2, L)
    for x in range(nx // 2):
        part[0, x, pl.ds(0, ny // 2, stride=2), :] = q[x]
        part[0, x, pl.ds(1, ny // 2, stride=2), :] = q[x]
    t = part[0]
    v = v + jnp.concatenate([t[:, None], t[:, None]], 1).reshape(nx, ny, L)
    for colour in (0, 1, 0, 1):
        v = sweep(v, colour)
    return v


def whole_kernel(level, group, f_in, c_in, out, *scratch):
    out[...] = whole_cycle(level, f_in[...], c_in[...], group, scratch)


def coefs_kernel(c_in, *refs):
    outs, parts = refs[: len(refs) // 2], refs[len(refs) // 2 :]
    source = c_in
    for out, part in zip(outs, parts):
        for a in range(part.shape[0]):
            for x in range(part.shape[1]):
                part[a, x] = source[a, 2 * x] + source[a, 2 * x + 1]
        for a, g in enumerate(fold(part, 0, part.shape[2] // 2)):
            out[a] = g
        source = out


def call(kernel, inputs, outs, scratch):
    one = not isinstance(outs, list)
    shapes = [jax.ShapeDtypeStruct(s, jnp.float32) for s in ([outs] if one else outs)]
    result = pl.pallas_call(
        kernel,
        out_shape=shapes,
        in_specs=[VMEM] * len(inputs),
        out_specs=[VMEM] * len(shapes),
        scratch_shapes=[pltpu.VMEM(s, jnp.float32) for s in scratch],
        compiler_params=pltpu.CompilerParams(vmem_limit_bytes=48 * 1024 * 1024),
    )(*inputs)
    return result[0] if one else result


def shift(block, axis, step):
    count = lax.axis_size(axis)
    return lax.ppermute(block, axis, [(i, (i + step) % count) for i in range(count)])


def with_halo(arrays):
    counts = [a.shape[0] for a in arrays]

    def joined(cut):
        return jnp.concatenate([cut(a) for a in arrays], 0)

    x_low = shift(joined(lambda a: a[:, -W:]), "gx", 1)
    x_high = shift(joined(lambda a: a[:, :W]), "gx", -1)
    y_low = shift(joined(lambda a: a[:, :, -W:]), "gy", 1)
    y_high = shift(joined(lambda a: a[:, :, :W]), "gy", -1)
    sides = jnp.concatenate([y_low, y_high], 2)
    c_low = shift(sides[:, -W:], "gx", 1)
    c_high = shift(sides[:, :W], "gx", -1)
    results, at = [], 0
    for a, n in zip(arrays, counts):
        s = slice(at, at + n)
        at += n
        low = jnp.concatenate([c_low[s, :, :W], y_low[s], c_high[s, :, :W]], 1)
        high = jnp.concatenate([c_low[s, :, W:], y_high[s], c_high[s, :, W:]], 1)
        middle = jnp.concatenate([x_low[s], a, x_high[s]], 1)
        results.append(jnp.concatenate([low, middle, high], 2))
    return results


def gathered(own):
    whole = lax.all_gather(own[:, :, : L // 2], ("gx", "gy"))
    nx, ny = lax.axis_size("gx"), lax.axis_size("gy")
    whole = whole.reshape((nx, ny) + own.shape[:2] + (L // 2,)).transpose(0, 2, 1, 3, 4)
    whole = whole.reshape(nx * own.shape[0], ny * own.shape[1], L // 2)
    return jnp.pad(whole, ((0, 0), (0, 0), (0, L // 2)))


def local(rhs, coefficient):
    shapes = [rhs.shape]
    for _ in range(SPLIT):
        k, a, b, c = shapes[-1]
        shapes.append(((k + 1) // 2, a // 2, b // 2, L))

    def extended(shape):
        return (shape[0], shape[1] + 2 * W, shape[2] + 2 * W, L)

    coarser = call(
        coefs_kernel, [coefficient], shapes[1:],
        [(s[0], s[1] // 2, s[2], L) for s in shapes[:-1]],
    )
    coefs = [coefficient] + list(coarser)
    coef_whole = gathered(coefs[SPLIT][0])

    source = rhs
    fields, kept = [], []
    for level in range(SPLIT):
        shape = shapes[level]
        ext = extended(shape)
        if level == 0:
            f_ext, c_ext = with_halo([source, coefficient])
        else:
            (f_ext,) = with_halo([source])
            (c_ext,) = with_halo([coefs[level]])
        fd, w, v, source = call(
            functools.partial(down_kernel, 0.25**level, L >> level), [f_ext, c_ext],
            [ext, ext, shape, shapes[level + 1]],
            [ext, (shape[0], shape[1] // 2, ext[2], L)],
        )
        fields.append(v)
        kept.append((fd, w))

    group = L >> SPLIT
    f_whole = gathered(source[0])
    scratch = []
    nx, ny = f_whole.shape[0], f_whole.shape[1]
    for level in range(SPLIT, LEVELS - 1):
        scratch.append((1, nx // 2, ny, L))
        nx, ny = nx // 2, ny // 2
    e = call(functools.partial(whole_kernel, SPLIT, group), [f_whole, coef_whole], f_whole.shape, scratch)

    h = W // 2
    e = jnp.concatenate([e[-h:], e, e[:h]], 0)
    e = jnp.concatenate([e[:, -h:], e, e[:, :h]], 1)
    sx, sy = shapes[SPLIT][1], shapes[SPLIT][2]
    e = lax.dynamic_slice(
        e, (lax.axis_index("gx") * sx, lax.axis_index("gy") * sy, 0), (sx + 2 * h, sy + 2 * h, L)
    )
    level = SPLIT - 1
    (t_ext,) = with_halo([fields[level]])
    ext = extended(shapes[level])
    t = call(
        functools.partial(up_last_kernel, 0.25**level, L >> level),
        [t_ext, e, *kept[level], fields[level - 1]], shapes[level - 1],
        [ext, (sx + 2 * h, ext[2], L), (shapes[level][1], 2 * shapes[level][2], L)],
    )
    for level in range(SPLIT - 2, -1, -1):
        (t_ext,) = with_halo([t])
        inputs = [t_ext, *kept[level]]
        ext, shape = extended(shapes[level]), shapes[level]
        if level:
            t = call(
                functools.partial(up_kernel, 0.25**level, L >> level), inputs + [fields[level - 1]],
                shapes[level - 1], [ext, (shape[1], 2 * shape[2], L)],
            )
        else:
            t = call(functools.partial(up_kernel, 1.0, L), inputs, shape, [ext])
    return t


def solution(mesh):
    spec = P(None, "gx", "gy", None)
    return jax.shard_map(local, mesh=mesh, in_specs=(spec, spec), out_specs=spec, check_vma=False)
```

```python
import functools
import jax
import jax.numpy as jnp
import numpy as np
from jax import lax
from jax.experimental import pallas as pl
from jax.experimental.pallas import tpu as pltpu
from jax.sharding import PartitionSpec as P

LEVELS = 6
SPLIT = 3
W = 4
L = 128
VMEM = pl.BlockSpec(memory_space=pltpu.VMEM)


def iota(shape, dim):
    return lax.broadcasted_iota(jnp.int32, shape, dim)


def z_sum(v, group):
    axis = v.ndim - 1
    if group == L:
        return pltpu.roll(v, 1, axis) + pltpu.roll(v, L - 1, axis)
    place = iota(v.shape, axis) % group
    up = jnp.where(place == group - 1, pltpu.roll(v, group - 1, axis), pltpu.roll(v, L - 1, axis))
    down = jnp.where(place == 0, pltpu.roll(v, L - group + 1, axis), pltpu.roll(v, 1, axis))
    return up + down


def y_sum(v):
    axis, n = v.ndim - 2, v.shape[-2]
    return pltpu.roll(v, 1, axis) + pltpu.roll(v, n - 1, axis)


def squeeze_matrix(half, scale):
    source, target = iota((L, L), 0), iota((L, L), 1)
    return jnp.where(target == source // 2 + half * (L // 2), scale, 0.0).astype(jnp.float32)


def spread_matrix(half):
    source, target = iota((L, L), 0), iota((L, L), 1)
    return jnp.where(source == target // 2 + half * (L // 2), 1.0, 0.0).astype(jnp.float32)


def dot(a, b):
    return jnp.dot(a, b, preferred_element_type=jnp.float32, precision=lax.Precision.HIGHEST)


def fold(part, first, rows):
    count, nx = part.shape[0], part.shape[1]
    outs = []
    for a in range(0, count, 2):
        total = None
        for h in range(min(2, count - a)):
            m = squeeze_matrix(h, 0.125)
            even = jnp.concatenate([part[a + h, x, pl.ds(first, rows, stride=2), :] for x in range(nx)], 0)
            odd = jnp.concatenate([part[a + h, x, pl.ds(first + 1, rows, stride=2), :] for x in range(nx)], 0)
            term = dot(even + odd, m)
            total = term if total is None else total + term
        outs.append(total.reshape(nx, rows, L))
    return outs


def half_sweep(v, f_ref, w_ref, colour, low, high, group):
    count, rows = v.shape[0], v.shape[2]
    parity = (iota((rows, L), 0) + iota((rows, L), 1)) % 2

    def body(step, carry):
        for k in range(2):
            x = low + 2 * step + k
            mask = parity == (colour + low + k) % 2
            for c in range(count):
                mid = v[c, x]
                total = v[c, x - 1] + v[c, x + 1] + y_sum(mid) + z_sum(mid, group)
                v[c, x] = jnp.where(mask, f_ref[c, x] + w_ref[c, x] * total, mid)
        return carry

    lax.fori_loop(0, (high - low) // 2, body, 0)


def down_kernel(scale, group, f_in, c_in, f_out, w_out, v_out, g_out, v, part):
    count, nx, ny = v_out.shape[0], v_out.shape[1], v_out.shape[2]
    ex = f_in.shape[1]
    rows = f_in.shape[2]
    parity = (iota((rows, L), 0) + iota((rows, L), 1)) % 2

    def first(step, carry):
        for k in range(2):
            x = 2 * step + k
            for c in range(count):
                inverse = 1.0 / (c_in[c, x] + 6.0 * scale)
                fd = f_in[c, x] * inverse
                f_out[c, x] = fd
                w_out[c, x] = scale * inverse
                v[c, x] = jnp.where(parity == k, fd, 0.0)
        return carry

    lax.fori_loop(0, ex // 2, first, 0)
    half_sweep(v, f_out, w_out, 1, 1, ex - 1, group)
    half_sweep(v, f_out, w_out, 0, 2, ex - 2, group)
    half_sweep(v, f_out, w_out, 1, 3, ex - 3, group)

    def last(step, carry):
        for c in range(count):
            total = None
            for k in range(2):
                x = W + 2 * step + k
                mid = v[c, x]
                nb = v[c, x - 1] + v[c, x + 1] + y_sum(mid) + z_sum(mid, group)
                r = f_in[c, x] - (c_in[c, x] * mid + scale * (6.0 * mid - nb))
                v_out[c, 2 * step + k] = v[c, x, W : W + ny, :]
                total = r if total is None else total + r
            part[c, step] = total
        return carry

    lax.fori_loop(0, nx // 2, last, 0)
    for a, g in enumerate(fold(part, W, ny // 2)):
        g_out[a] = g


def spread(e, half, t):
    q = dot(e, spread_matrix(half))
    n = q.shape[0]
    t[pl.ds(0, n, stride=2), :] = q
    t[pl.ds(1, n, stride=2), :] = q


def post(v, f_ref, w_ref, group):
    ex = v.shape[1]
    for p, colour in ((1, 0), (2, 1), (3, 0), (4, 1)):
        half_sweep(v, f_ref, w_ref, colour, p, ex - p, group)


def up_kernel(scale, group, t_in, f_in, w_in, *rest):
    if len(rest) == 2:
        out, v = rest
        fine = None
    else:
        fine, out, v, t = rest
    ex = t_in.shape[1]

    def copy(x, carry):
        for c in range(t_in.shape[0]):
            v[c, x] = t_in[c, x]
        return carry

    lax.fori_loop(0, ex, copy, 0)
    finish(v, f_in, w_in, group, fine, out, None if fine is None else t)


def finish(v, f_in, w_in, group, fine, out, t):
    post(v, f_in, w_in, group)
    ex, ey = v.shape[1], v.shape[2]
    nx, ny = ex - 2 * W, ey - 2 * W
    if fine is None:

        def give(x, carry):
            for c in range(v.shape[0]):
                out[c, x] = v[c, W + x, W : W + ny, :]
            return carry

        lax.fori_loop(0, nx, give, 0)
        return
    for c in range(v.shape[0]):
        for h in range(2):
            q = dot(v[c, W : W + nx, W : W + ny, :].reshape(nx * ny, L), spread_matrix(h)).reshape(nx, ny, L)
            for x in range(nx):
                t[x, pl.ds(0, ny, stride=2), :] = q[x]
                t[x, pl.ds(1, ny, stride=2), :] = q[x]
            for x in range(nx):
                for k in range(2):
                    out[2 * c + h, 2 * x + k] = fine[2 * c + h, 2 * x + k] + t[x]


def up_last_kernel(scale, group, t_in, e_in, f_in, w_in, fine, out, v, te, t):
    for i in range(e_in.shape[0]):
        q = dot(e_in[i], spread_matrix(0))
        n = q.shape[0]
        te[i, pl.ds(0, n, stride=2), :] = q
        te[i, pl.ds(1, n, stride=2), :] = q
        for k in range(2):
            v[0, 2 * i + k] = t_in[0, 2 * i + k] + te[i]
    finish(v, f_in, w_in, group, fine, out, t)


def whole_neighbours(v, group):
    up = jnp.concatenate([v[1:], v[:1]], 0)
    down = jnp.concatenate([v[-1:], v[:-1]], 0)
    return up + down + y_sum(v) + z_sum(v, group)


def whole_cycle(level, f, coef, group, scratch):
    scale = 0.25**level
    inverse = 1.0 / (coef + 6.0 * scale)
    fd, w = f * inverse, scale * inverse
    parity = (iota(f.shape, 0) + iota(f.shape, 1) + iota(f.shape, 2)) % 2

    def sweep(v, colour):
        return jnp.where(parity == colour, fd + w * whole_neighbours(v, group), v)

    v = jnp.where(parity == 0, fd, 0.0)
    v = sweep(sweep(sweep(v, 1), 0), 1)
    if level == LEVELS - 1:
        return v
    part = scratch[0]
    nx, ny = f.shape[0], f.shape[1]

    def coarse(u):
        pairs = u.reshape(nx // 2, 2, ny, L)
        part[0] = pairs[:, 0] + pairs[:, 1]
        return fold(part, 0, ny // 2)[0]

    g = coarse(f - (coef * v + scale * (6.0 * v - whole_neighbours(v, group))))
    c = coarse(coef)
    e = whole_cycle(level + 1, g, c, group // 2, scratch[1:])
    q = dot(e.reshape(nx // 2 * (ny // 2), L), spread_matrix(0)).reshape(nx // 2, ny // 2, L)
    for x in range(nx // 2):
        part[0, x, pl.ds(0, ny // 2, stride=2), :] = q[x]
        part[0, x, pl.ds(1, ny // 2, stride=2), :] = q[x]
    t = part[0]
    v = v + jnp.concatenate([t[:, None], t[:, None]], 1).reshape(nx, ny, L)
    for colour in (0, 1, 0, 1):
        v = sweep(v, colour)
    return v


def whole_kernel(level, group, f_in, c_in, out, *scratch):
    out[...] = whole_cycle(level, f_in[...], c_in[...], group, scratch)


def coefs_kernel(c_in, *refs):
    outs, parts = refs[: len(refs) // 2], refs[len(refs) // 2 :]
    source = c_in
    for out, part in zip(outs, parts):
        for a in range(part.shape[0]):
            for x in range(part.shape[1]):
                part[a, x] = source[a, 2 * x] + source[a, 2 * x + 1]
        for a, g in enumerate(fold(part, 0, part.shape[2] // 2)):
            out[a] = g
        source = out


def call(kernel, inputs, outs, scratch):
    one = not isinstance(outs, list)
    shapes = [jax.ShapeDtypeStruct(s, jnp.float32) for s in ([outs] if one else outs)]
    result = pl.pallas_call(
        kernel,
        out_shape=shapes,
        in_specs=[VMEM] * len(inputs),
        out_specs=[VMEM] * len(shapes),
        scratch_shapes=[pltpu.VMEM(s, jnp.float32) for s in scratch],
        compiler_params=pltpu.CompilerParams(vmem_limit_bytes=48 * 1024 * 1024),
    )(*inputs)
    return result[0] if one else result


def remote_call(kernel, inputs, outs, scratch, copies, collective_id):
    return pl.pallas_call(
        kernel,
        out_shape=[jax.ShapeDtypeStruct(s, jnp.float32) for s in outs],
        in_specs=[VMEM] * len(inputs),
        out_specs=[VMEM] * len(outs),
        scratch_shapes=[pltpu.VMEM(s, jnp.float32) for s in scratch]
        + [pltpu.SemaphoreType.DMA((copies,)), pltpu.SemaphoreType.DMA((copies,))],
        compiler_params=pltpu.CompilerParams(
            vmem_limit_bytes=48 * 1024 * 1024, collective_id=collective_id, has_side_effects=True
        ),
    )(*inputs)


def greet(devices):
    barrier = pltpu.get_barrier_semaphore()
    for device in devices:
        pl.semaphore_signal(barrier, inc=1, device_id=device, device_id_type=pl.DeviceIdType.MESH)
    return barrier, len(devices)


SIDES = [(-1, 0), (1, 0), (0, -1), (0, 1), (-1, -1), (-1, 1), (1, -1), (1, 1)]


def merged(v):
    pairs = v.reshape((v.shape[0] // 2, 2) + v.shape[1:])
    odd = (iota(v.shape[1:], 0) + iota(v.shape[1:], 1)) % 2 == 1
    return jnp.where(odd, pairs[:, 0], pairs[:, 1])


def doubled(m):
    return jnp.concatenate([m[:, None], m[:, None]], 1).reshape((2 * m.shape[0],) + m.shape[1:])


def halo_kernel(dims, merge, n, *refs):
    ins, outs = refs[:n], refs[n : 2 * n]
    xs, ys, xr, yr, cr, send_sem, recv_sem = refs[2 * n :]
    nx, ny = ins[0].shape[1], ins[0].shape[2]
    me_x, me_y = lax.axis_index("gx"), lax.axis_index("gy")
    devices = [
        (lax.rem(me_x + dx + dims[0], dims[0]), lax.rem(me_y + dy + dims[1], dims[1])) for dx, dy in SIDES
    ]
    barrier, count = greet(devices)
    pack = merged if merge else lambda v: v
    unpack = doubled if merge else lambda v: v
    at = 0
    for ref in ins:
        for c in range(ref.shape[0]):
            xs[0, at] = pack(ref[c, 0:W])
            xs[1, at] = pack(ref[c, nx - W : nx])
            ys[0, at] = pack(ref[c, :, 0:W, :])
            ys[1, at] = pack(ref[c, :, ny - W : ny, :])
            at += 1
    pl.semaphore_wait(barrier, count)
    w, long = xs.shape[2], ys.shape[2]
    copies = []
    for k, (dx, dy) in enumerate(SIDES):
        sx, sy = int(dx > 0), int(dy > 0)
        if dy == 0:
            source, target = xs.at[sx], xr.at[sx]
        elif dx == 0:
            source, target = ys.at[sy], yr.at[sy]
        else:
            source, target = ys.at[sy, :, pl.ds((long - w) * sx, w)], cr.at[sx, sy]
        copies.append(
            pltpu.make_async_remote_copy(
                src_ref=source, dst_ref=target, send_sem=send_sem.at[k], recv_sem=recv_sem.at[k],
                device_id=devices[k], device_id_type=pl.DeviceIdType.MESH,
            )
        )
    for copy in copies:
        copy.start()
    for ref, out in zip(ins, outs):
        for c in range(ref.shape[0]):
            out[c, W : W + nx, W : W + ny, :] = ref[c]
    for copy in copies:
        copy.wait()
    at = 0
    for out in outs:
        for c in range(out.shape[0]):
            for s in range(2):
                first_x, first_y = (W + nx, W + ny) if s == 0 else (0, 0)
                out[c, first_x : first_x + W, W : W + ny, :] = unpack(xr[s, at])
                out[c, W : W + nx, first_y : first_y + W, :] = unpack(yr[s, at])
                for u in range(2):
                    corner = W + ny if u == 0 else 0
                    out[c, first_x : first_x + W, corner : corner + W, :] = unpack(cr[s, u, at])
            at += 1


def with_halo(dims, arrays, collective_id, merge=False):
    count = sum(a.shape[0] for a in arrays)
    nx, ny = arrays[0].shape[1], arrays[0].shape[2]
    w, long = (W // 2, nx // 2) if merge else (W, nx)
    flat, tall = (2, count, w, ny, L), (2, count, long, W, L)
    return remote_call(
        functools.partial(halo_kernel, dims, merge, len(arrays)), arrays,
        [(a.shape[0], nx + 2 * W, ny + 2 * W, L) for a in arrays],
        [flat, tall, flat, tall, (2, 2, count, w, W, L)], len(SIDES), collective_id,
    )


def gather_kernel(dims, f_in, c_in, f_out, c_out, slots, send_sem, recv_sem):
    me_x, me_y = lax.axis_index("gx"), lax.axis_index("gy")
    along_x = [(lax.rem(me_x + d, dims[0]), me_y) for d in range(1, dims[0])]
    along_y = [(me_x, lax.rem(me_y + d, dims[1])) for d in range(1, dims[1])]
    barrier, count = greet(along_x + along_y)
    half = iota(f_in.shape, 2) < L // 2
    slots[me_y, me_x] = jnp.where(half, f_in[...], pltpu.roll(c_in[...], L // 2, 2))
    pl.semaphore_wait(barrier, count)
    at = 0
    for devices, part in ((along_x, slots.at[me_y, me_x]), (along_y, slots.at[me_y])):
        copies = []
        for device in devices:
            copies.append(
                pltpu.make_async_remote_copy(
                    src_ref=part, dst_ref=part, send_sem=send_sem.at[at], recv_sem=recv_sem.at[at],
                    device_id=device, device_id_type=pl.DeviceIdType.MESH,
                )
            )
            at += 1
        for copy in copies:
            copy.start()
        for copy in copies:
            copy.wait()
    rows, ny = f_out.shape[0], f_in.shape[1]
    for j in range(dims[1]):
        part = slots[j].reshape(rows, ny, L)
        low = iota(part.shape, 2) < L // 2
        f_out[:, j * ny : (j + 1) * ny, :] = jnp.where(low, part, 0.0)
        c_out[:, j * ny : (j + 1) * ny, :] = jnp.where(low, pltpu.roll(part, L // 2, 2), 0.0)


def gathered(dims, f, coef, collective_id):
    shape = (f.shape[0] * dims[0], f.shape[1] * dims[1], L)
    return remote_call(
        functools.partial(gather_kernel, dims), [f, coef], [shape, shape],
        [(dims[1], dims[0]) + f.shape], dims[0] + dims[1] - 2, collective_id,
    )


def local(dims, rhs, coefficient):
    shapes = [rhs.shape]
    for _ in range(SPLIT):
        k, a, b, c = shapes[-1]
        shapes.append(((k + 1) // 2, a // 2, b // 2, L))

    def extended(shape):
        return (shape[0], shape[1] + 2 * W, shape[2] + 2 * W, L)

    coarser = call(
        coefs_kernel, [coefficient], shapes[1:],
        [(s[0], s[1] // 2, s[2], L) for s in shapes[:-1]],
    )
    coefs = [coefficient] + list(coarser)

    source = rhs
    fields, kept = [], []
    for level in range(SPLIT):
        shape = shapes[level]
        ext = extended(shape)
        f_ext, c_ext = with_halo(dims, [source, coefs[level]], level)
        fd, w, v, source = call(
            functools.partial(down_kernel, 0.25**level, L >> level), [f_ext, c_ext],
            [ext, ext, shape, shapes[level + 1]],
            [ext, (shape[0], shape[1] // 2, ext[2], L)],
        )
        fields.append(v)
        kept.append((fd, w))

    group = L >> SPLIT
    f_whole, coef_whole = gathered(dims, source[0], coefs[SPLIT][0], 2 * SPLIT)
    scratch = []
    nx, ny = f_whole.shape[0], f_whole.shape[1]
    for level in range(SPLIT, LEVELS - 1):
        scratch.append((1, nx // 2, ny, L))
        nx, ny = nx // 2, ny // 2
    e = call(functools.partial(whole_kernel, SPLIT, group), [f_whole, coef_whole], f_whole.shape, scratch)

    h = W // 2
    e = jnp.concatenate([e[-h:], e, e[:h]], 0)
    e = jnp.concatenate([e[:, -h:], e, e[:, :h]], 1)
    sx, sy = shapes[SPLIT][1], shapes[SPLIT][2]
    e = lax.dynamic_slice(
        e, (lax.axis_index("gx") * sx, lax.axis_index("gy") * sy, 0), (sx + 2 * h, sy + 2 * h, L)
    )
    level = SPLIT - 1
    (t_ext,) = with_halo(dims, [fields[level]], SPLIT + level, True)
    ext = extended(shapes[level])
    t = call(
        functools.partial(up_last_kernel, 0.25**level, L >> level),
        [t_ext, e, *kept[level], fields[level - 1]], shapes[level - 1],
        [ext, (sx + 2 * h, ext[2], L), (shapes[level][1], 2 * shapes[level][2], L)],
    )
    for level in range(SPLIT - 2, -1, -1):
        (t_ext,) = with_halo(dims, [t], SPLIT + level, True)
        inputs = [t_ext, *kept[level]]
        ext, shape = extended(shapes[level]), shapes[level]
        if level:
            t = call(
                functools.partial(up_kernel, 0.25**level, L >> level), inputs + [fields[level - 1]],
                shapes[level - 1], [ext, (shape[1], 2 * shape[2], L)],
            )
        else:
            t = call(functools.partial(up_kernel, 1.0, L), inputs, shape, [ext])
    return t


def solution(mesh):
    spec = P(None, "gx", "gy", None)
    dims = (mesh.shape["gx"], mesh.shape["gy"])
    return jax.shard_map(functools.partial(local, dims), mesh=mesh, in_specs=(spec, spec), out_specs=spec, check_vma=False)
```

```python
import functools
import jax
import jax.numpy as jnp
import numpy as np
from jax import lax
from jax.experimental import pallas as pl
from jax.experimental.pallas import tpu as pltpu
from jax.sharding import PartitionSpec as P

LEVELS = 6
SPLIT = 3
W = 4
L = 128
VMEM = pl.BlockSpec(memory_space=pltpu.VMEM)


def iota(shape, dim):
    return lax.broadcasted_iota(jnp.int32, shape, dim)


def z_sum(v, group):
    axis = v.ndim - 1
    if group == L:
        return pltpu.roll(v, 1, axis) + pltpu.roll(v, L - 1, axis)
    place = iota(v.shape, axis) % group
    up = jnp.where(place == group - 1, pltpu.roll(v, group - 1, axis), pltpu.roll(v, L - 1, axis))
    down = jnp.where(place == 0, pltpu.roll(v, L - group + 1, axis), pltpu.roll(v, 1, axis))
    return up + down


def y_sum(v):
    axis, n = v.ndim - 2, v.shape[-2]
    return pltpu.roll(v, 1, axis) + pltpu.roll(v, n - 1, axis)


def squeeze_matrix(half, scale):
    source, target = iota((L, L), 0), iota((L, L), 1)
    return jnp.where(target == source // 2 + half * (L // 2), scale, 0.0).astype(jnp.float32)


def spread_matrix(half):
    source, target = iota((L, L), 0), iota((L, L), 1)
    return jnp.where(source == target // 2 + half * (L // 2), 1.0, 0.0).astype(jnp.float32)


def dot(a, b):
    return jnp.dot(a, b, preferred_element_type=jnp.float32, precision=lax.Precision.HIGHEST)


def fold(part, first, rows):
    count, nx = part.shape[0], part.shape[1]
    outs = []
    for a in range(0, count, 2):
        total = None
        for h in range(min(2, count - a)):
            m = squeeze_matrix(h, 0.125)
            even = jnp.concatenate([part[a + h, x, pl.ds(first, rows, stride=2), :] for x in range(nx)], 0)
            odd = jnp.concatenate([part[a + h, x, pl.ds(first + 1, rows, stride=2), :] for x in range(nx)], 0)
            term = dot(even + odd, m)
            total = term if total is None else total + term
        outs.append(total.reshape(nx, rows, L))
    return outs


def half_sweep(v, f_ref, w_ref, colour, low, high, group, comps=None):
    rows = v.shape[2]
    comps = range(v.shape[0]) if comps is None else comps
    parity = (iota((rows, L), 0) + iota((rows, L), 1)) % 2
    at_once = 4 if len(comps) == 1 else 2

    def some(start, count):
        for k in range(count):
            x = start + k
            mask = parity == (colour + low + k) % 2
            for c in comps:
                mid = v[c, x]
                total = v[c, x - 1] + v[c, x + 1] + y_sum(mid) + z_sum(mid, group)
                v[c, x] = jnp.where(mask, f_ref[c, x] + w_ref[c, x] * total, mid)

    def body(step, carry):
        some(low + at_once * step, at_once)
        return carry

    steps, left = divmod(high - low, at_once)
    lax.fori_loop(0, steps, body, 0)
    if left:
        some(high - left, left)


def down_kernel(scale, group, f_in, c_in, f_out, w_out, v_out, g_out, v, part):
    down(scale, group, range(v.shape[0]), f_in, c_in, f_out, w_out, v_out, v, part)
    for a, g in enumerate(fold(part, W, v_out.shape[2] // 2)):
        g_out[a] = g


def down(scale, group, comps, f_in, c_in, f_out, w_out, v_out, v, part):
    nx, ny = v_out.shape[1], v_out.shape[2]
    ex, rows = f_in.shape[1], f_in.shape[2]
    parity = (iota((rows, L), 0) + iota((rows, L), 1)) % 2

    def first(step, carry):
        for k in range(2):
            x = 2 * step + k
            for c in comps:
                inverse = 1.0 / (c_in[c, x] + 6.0 * scale)
                fd = f_in[c, x] * inverse
                f_out[c, x] = fd
                w_out[c, x] = scale * inverse
                v[c, x] = jnp.where(parity == k, fd, 0.0)
        return carry

    lax.fori_loop(0, ex // 2, first, 0)
    half_sweep(v, f_out, w_out, 1, 1, ex - 1, group, comps)
    half_sweep(v, f_out, w_out, 0, 2, ex - 2, group, comps)
    half_sweep(v, f_out, w_out, 1, 3, ex - 3, group, comps)

    def last(step, carry):
        for c in comps:
            total = None
            for k in range(2):
                x = W + 2 * step + k
                mid = v[c, x]
                nb = v[c, x - 1] + v[c, x + 1] + y_sum(mid) + z_sum(mid, group)
                r = f_in[c, x] - (c_in[c, x] * mid + scale * (6.0 * mid - nb))
                v_out[c, 2 * step + k] = v[c, x, W : W + ny, :]
                total = r if total is None else total + r
            part[c, step] = total
        return carry

    lax.fori_loop(0, nx // 2, last, 0)


def post(v, f_ref, w_ref, group, comps=None):
    ex = v.shape[1]
    for p, colour in ((1, 0), (2, 1), (3, 0), (4, 1)):
        half_sweep(v, f_ref, w_ref, colour, p, ex - p, group, comps)


def up_kernel(scale, group, t_in, f_in, w_in, fine, out, v, t):
    def copy(x, carry):
        for c in range(t_in.shape[0]):
            v[c, x] = t_in[c, x]
        return carry

    lax.fori_loop(0, t_in.shape[1], copy, 0)
    finish(v, f_in, w_in, group, fine, out, t)


def finish(v, f_in, w_in, group, fine, out, t):
    post(v, f_in, w_in, group)
    ex, ey = v.shape[1], v.shape[2]
    nx, ny = ex - 2 * W, ey - 2 * W
    for c in range(v.shape[0]):
        for h in range(2):
            q = dot(v[c, W : W + nx, W : W + ny, :].reshape(nx * ny, L), spread_matrix(h)).reshape(nx, ny, L)
            for x in range(nx):
                t[x, pl.ds(0, ny, stride=2), :] = q[x]
                t[x, pl.ds(1, ny, stride=2), :] = q[x]
            for x in range(nx):
                for k in range(2):
                    out[2 * c + h, 2 * x + k] = fine[2 * c + h, 2 * x + k] + t[x]


def up_last_kernel(scale, group, t_in, e_in, f_in, w_in, fine, out, v, te, t):
    for i in range(e_in.shape[0]):
        q = dot(e_in[i], spread_matrix(0))
        n = q.shape[0]
        te[i, pl.ds(0, n, stride=2), :] = q
        te[i, pl.ds(1, n, stride=2), :] = q
        for k in range(2):
            v[0, 2 * i + k] = t_in[0, 2 * i + k] + te[i]
    finish(v, f_in, w_in, group, fine, out, t)


def whole_neighbours(v, group):
    up = jnp.concatenate([v[1:], v[:1]], 0)
    down = jnp.concatenate([v[-1:], v[:-1]], 0)
    return up + down + y_sum(v) + z_sum(v, group)


def whole_cycle(level, f, coef, group, scratch):
    scale = 0.25**level
    inverse = 1.0 / (coef + 6.0 * scale)
    fd, w = f * inverse, scale * inverse
    parity = (iota(f.shape, 0) + iota(f.shape, 1) + iota(f.shape, 2)) % 2

    def sweep(v, colour):
        return jnp.where(parity == colour, fd + w * whole_neighbours(v, group), v)

    v = jnp.where(parity == 0, fd, 0.0)
    v = sweep(sweep(sweep(v, 1), 0), 1)
    if level == LEVELS - 1:
        return v
    part = scratch[0]
    nx, ny = f.shape[0], f.shape[1]

    def coarse(u):
        pairs = u.reshape(nx // 2, 2, ny, L)
        part[0] = pairs[:, 0] + pairs[:, 1]
        return fold(part, 0, ny // 2)[0]

    g = coarse(f - (coef * v + scale * (6.0 * v - whole_neighbours(v, group))))
    c = coarse(coef)
    e = whole_cycle(level + 1, g, c, group // 2, scratch[1:])
    q = dot(e.reshape(nx // 2 * (ny // 2), L), spread_matrix(0)).reshape(nx // 2, ny // 2, L)
    for x in range(nx // 2):
        part[0, x, pl.ds(0, ny // 2, stride=2), :] = q[x]
        part[0, x, pl.ds(1, ny // 2, stride=2), :] = q[x]
    t = part[0]
    v = v + jnp.concatenate([t[:, None], t[:, None]], 1).reshape(nx, ny, L)
    for colour in (0, 1, 0, 1):
        v = sweep(v, colour)
    return v


def whole_kernel(level, group, f_in, c_in, out, *scratch):
    out[...] = whole_cycle(level, f_in[...], c_in[...], group, scratch)


def coefs_kernel(c_in, *refs):
    outs, parts = refs[: len(refs) // 2], refs[len(refs) // 2 :]
    source = c_in
    for out, part in zip(outs, parts):
        for a in range(part.shape[0]):
            for x in range(part.shape[1]):
                part[a, x] = source[a, 2 * x] + source[a, 2 * x + 1]
        for a, g in enumerate(fold(part, 0, part.shape[2] // 2)):
            out[a] = g
        source = out


def call(kernel, inputs, outs, scratch):
    one = not isinstance(outs, list)
    shapes = [jax.ShapeDtypeStruct(s, jnp.float32) for s in ([outs] if one else outs)]
    result = pl.pallas_call(
        kernel,
        out_shape=shapes,
        in_specs=[VMEM] * len(inputs),
        out_specs=[VMEM] * len(shapes),
        scratch_shapes=[pltpu.VMEM(s, jnp.float32) for s in scratch],
        compiler_params=pltpu.CompilerParams(vmem_limit_bytes=48 * 1024 * 1024),
    )(*inputs)
    return result[0] if one else result


def remote_call(kernel, inputs, outs, scratch, copies, collective_id):
    return pl.pallas_call(
        kernel,
        out_shape=[jax.ShapeDtypeStruct(s, jnp.float32) for s in outs],
        in_specs=[VMEM] * len(inputs),
        out_specs=[VMEM] * len(outs),
        scratch_shapes=[pltpu.VMEM(s, jnp.float32) for s in scratch]
        + [pltpu.SemaphoreType.DMA((copies,)), pltpu.SemaphoreType.DMA((copies,))],
        compiler_params=pltpu.CompilerParams(
            vmem_limit_bytes=48 * 1024 * 1024, collective_id=collective_id, has_side_effects=True
        ),
    )(*inputs)


def greet(devices):
    barrier = pltpu.get_barrier_semaphore()
    for device in devices:
        pl.semaphore_signal(barrier, inc=1, device_id=device, device_id_type=pl.DeviceIdType.MESH)
    return barrier, len(devices)


SIDES = [(-1, 0), (1, 0), (0, -1), (0, 1), (-1, -1), (-1, 1), (1, -1), (1, 1)]


def merged(v):
    pairs = v.reshape((v.shape[0] // 2, 2) + v.shape[1:])
    odd = (iota(v.shape[1:], 0) + iota(v.shape[1:], 1)) % 2 == 1
    return jnp.where(odd, pairs[:, 0], pairs[:, 1])


def doubled(m):
    return jnp.concatenate([m[:, None], m[:, None]], 1).reshape((2 * m.shape[0],) + m.shape[1:])


def ring(dims):
    me_x, me_y = lax.axis_index("gx"), lax.axis_index("gy")
    return [
        (lax.rem(me_x + dx + dims[0], dims[0]), lax.rem(me_y + dy + dims[1], dims[1])) for dx, dy in SIDES
    ]


BUFFERS = 7


def halo_scratch(count, nx, ny, merge):
    w, long = (W // 2, nx // 2) if merge else (W, nx)
    flat, tall = (2, count, w, ny, L), (2, count, long, W, L)
    shapes = [flat, tall, flat, tall, (2, 2, count, w, W, L)]
    return [pltpu.VMEM(s, jnp.float32) for s in shapes] + [pltpu.SemaphoreType.DMA((len(SIDES),))] * 2


class Halo:
    def __init__(self, devices, merge, sources, targets, buffers):
        self.merge, self.sources, self.targets = merge, sources, targets
        self.xs, self.ys, self.xr, self.yr, self.cr, send_sem, recv_sem = buffers
        self.nx, self.ny = sources[0][0].shape[1], sources[0][0].shape[2]
        w, long = self.xs.shape[2], self.ys.shape[2]
        self.copies = []
        for k, (dx, dy) in enumerate(SIDES):
            sx, sy = int(dx > 0), int(dy > 0)
            if dy == 0:
                source, target = self.xs.at[sx], self.xr.at[sx]
            elif dx == 0:
                source, target = self.ys.at[sy], self.yr.at[sy]
            else:
                source, target = self.ys.at[sy, :, pl.ds((long - w) * sx, w)], self.cr.at[sx, sy]
            self.copies.append(
                pltpu.make_async_remote_copy(
                    src_ref=source, dst_ref=target, send_sem=send_sem.at[k], recv_sem=recv_sem.at[k],
                    device_id=devices[k], device_id_type=pl.DeviceIdType.MESH,
                )
            )

    def stage(self):
        pack = merged if self.merge else lambda v: v
        nx, ny = self.nx, self.ny
        for at, (ref, c) in enumerate(self.sources):
            self.xs[0, at] = pack(ref[c, 0:W])
            self.xs[1, at] = pack(ref[c, nx - W : nx])
            self.ys[0, at] = pack(ref[c, :, 0:W, :])
            self.ys[1, at] = pack(ref[c, :, ny - W : ny, :])

    def start(self):
        for copy in self.copies:
            copy.start()

    def middle(self):
        for (ref, c), (out, d) in zip(self.sources, self.targets):
            out[d, W : W + self.nx, W : W + self.ny, :] = ref[c]

    def wait(self):
        for copy in self.copies:
            copy.wait()

    def edges(self):
        unpack = doubled if self.merge else lambda v: v
        nx, ny = self.nx, self.ny
        for at, (out, c) in enumerate(self.targets):
            for s in range(2):
                first_x, first_y = (W + nx, W + ny) if s == 0 else (0, 0)
                out[c, first_x : first_x + W, W : W + ny, :] = unpack(self.xr[s, at])
                out[c, W : W + nx, first_y : first_y + W, :] = unpack(self.yr[s, at])
                for u in range(2):
                    corner = W + ny if u == 0 else 0
                    out[c, first_x : first_x + W, corner : corner + W, :] = unpack(self.cr[s, u, at])


def pairs_of(refs):
    return [(ref, c) for ref in refs for c in range(ref.shape[0])]


def halo_kernel(dims, merge, n, *refs):
    devices = ring(dims)
    barrier, count = greet(devices)
    halo = Halo(devices, merge, pairs_of(refs[:n]), pairs_of(refs[n : 2 * n]), refs[2 * n :])
    halo.stage()
    pl.semaphore_wait(barrier, count)
    halo.start()
    halo.middle()
    halo.wait()
    halo.edges()


def in_turn(halos, work, tail):
    halos[0].start()
    for k, halo in enumerate(halos):
        if k + 1 < len(halos):
            halos[k + 1].stage()
        halo.middle()
        halo.wait()
        if k + 1 < len(halos):
            halos[k + 1].start()
        else:
            for other in tail:
                other.start()
        halo.edges()
        work(k)
    for other in tail:
        other.middle()
        other.wait()
        other.edges()


def first_down_kernel(dims, splits, *refs):
    f_in, c_in = refs[:2]
    coarse = refs[2 : 2 + splits]
    f_out, w_out, v_out, g_out = refs[2 + splits : 6 + splits]
    coarse_out = refs[6 + splits : 6 + 2 * splits]
    f_ext, c_ext, v, part = refs[6 + 2 * splits : 10 + 2 * splits]
    rest = refs[10 + 2 * splits :]
    devices = ring(dims)
    barrier, count = greet(devices)
    parts = f_in.shape[0]
    halos = [
        Halo(
            devices, False, [(f_in, c), (c_in, c)], [(f_ext, c), (c_ext, c)],
            rest[BUFFERS * c : BUFFERS * (c + 1)],
        )
        for c in range(parts)
    ]
    tail = [
        Halo(
            devices, False, pairs_of([coarse[i]]), pairs_of([coarse_out[i]]),
            rest[BUFFERS * (parts + i) : BUFFERS * (parts + i + 1)],
        )
        for i in range(splits)
    ]
    halos[0].stage()
    pl.semaphore_wait(barrier, count)
    for other in tail:
        other.stage()

    def work(c):
        down(1.0, L, [c], f_ext, c_ext, f_out, w_out, v_out, v, part)

    in_turn(halos, work, tail)
    for a, g in enumerate(fold(part, W, v_out.shape[2] // 2)):
        g_out[a] = g


def last_up_kernel(dims, t_in, f_in, w_in, out, v, *rest):
    devices = ring(dims)
    barrier, count = greet(devices)
    parts, nx, ny = out.shape[0], out.shape[1], out.shape[2]
    halos = [
        Halo(devices, True, [(t_in, c)], [(v, c)], rest[BUFFERS * c : BUFFERS * (c + 1)])
        for c in range(parts)
    ]
    halos[0].stage()
    pl.semaphore_wait(barrier, count)

    def work(c):
        post(v, f_in, w_in, L, [c])
        out[c] = v[c, W : W + nx, W : W + ny, :]

    in_turn(halos, work, [])


def remote_kernel(kernel, inputs, outs, scratch, collective_id):
    return pl.pallas_call(
        kernel,
        out_shape=[jax.ShapeDtypeStruct(s, jnp.float32) for s in outs],
        in_specs=[VMEM] * len(inputs),
        out_specs=[VMEM] * len(outs),
        scratch_shapes=scratch,
        compiler_params=pltpu.CompilerParams(
            vmem_limit_bytes=48 * 1024 * 1024, collective_id=collective_id, has_side_effects=True
        ),
    )(*inputs)


def with_halo(dims, arrays, collective_id, merge=False):
    count = sum(a.shape[0] for a in arrays)
    nx, ny = arrays[0].shape[1], arrays[0].shape[2]
    return remote_kernel(
        functools.partial(halo_kernel, dims, merge, len(arrays)), arrays,
        [(a.shape[0], nx + 2 * W, ny + 2 * W, L) for a in arrays],
        halo_scratch(count, nx, ny, merge), collective_id,
    )


def gather_kernel(dims, f_in, c_in, f_out, c_out, slots, send_sem, recv_sem):
    me_x, me_y = lax.axis_index("gx"), lax.axis_index("gy")
    along_x = [(lax.rem(me_x + d, dims[0]), me_y) for d in range(1, dims[0])]
    along_y = [(me_x, lax.rem(me_y + d, dims[1])) for d in range(1, dims[1])]
    barrier, count = greet(along_x + along_y)
    half = iota(f_in.shape, 2) < L // 2
    slots[me_y, me_x] = jnp.where(half, f_in[...], pltpu.roll(c_in[...], L // 2, 2))
    pl.semaphore_wait(barrier, count)
    at = 0
    for devices, part in ((along_x, slots.at[me_y, me_x]), (along_y, slots.at[me_y])):
        copies = []
        for device in devices:
            copies.append(
                pltpu.make_async_remote_copy(
                    src_ref=part, dst_ref=part, send_sem=send_sem.at[at], recv_sem=recv_sem.at[at],
                    device_id=device, device_id_type=pl.DeviceIdType.MESH,
                )
            )
            at += 1
        for copy in copies:
            copy.start()
        for copy in copies:
            copy.wait()
    rows, ny = f_out.shape[0], f_in.shape[1]
    for j in range(dims[1]):
        part = slots[j].reshape(rows, ny, L)
        low = iota(part.shape, 2) < L // 2
        f_out[:, j * ny : (j + 1) * ny, :] = jnp.where(low, part, 0.0)
        c_out[:, j * ny : (j + 1) * ny, :] = jnp.where(low, pltpu.roll(part, L // 2, 2), 0.0)


def gathered(dims, f, coef, collective_id):
    shape = (f.shape[0] * dims[0], f.shape[1] * dims[1], L)
    return remote_call(
        functools.partial(gather_kernel, dims), [f, coef], [shape, shape],
        [(dims[1], dims[0]) + f.shape], dims[0] + dims[1] - 2, collective_id,
    )


def local(dims, rhs, coefficient):
    shapes = [rhs.shape]
    for _ in range(SPLIT):
        k, a, b, c = shapes[-1]
        shapes.append(((k + 1) // 2, a // 2, b // 2, L))

    def extended(shape):
        return (shape[0], shape[1] + 2 * W, shape[2] + 2 * W, L)

    coarser = call(
        coefs_kernel, [coefficient], shapes[1:],
        [(s[0], s[1] // 2, s[2], L) for s in shapes[:-1]],
    )
    coefs = [coefficient] + list(coarser)

    source = rhs
    fields, kept = [], []
    for level in range(SPLIT):
        shape = shapes[level]
        ext = extended(shape)
        wide_part = (shape[0], shape[1] // 2, ext[2], L)
        if level == 0:
            scratch = [pltpu.VMEM(x, jnp.float32) for x in (ext, ext, ext, wide_part)]
            for _ in range(shape[0]):
                scratch += halo_scratch(2, shape[1], shape[2], False)
            for x in shapes[1:SPLIT]:
                scratch += halo_scratch(x[0], x[1], x[2], False)
            fd, w, v, source, *c_exts = remote_kernel(
                functools.partial(first_down_kernel, dims, SPLIT - 1), [source] + coefs[:SPLIT],
                [ext, ext, shape, shapes[1]] + [extended(x) for x in shapes[1:SPLIT]], scratch, 0,
            )
        else:
            (f_ext,) = with_halo(dims, [source], level)
            fd, w, v, source = call(
                functools.partial(down_kernel, 0.25**level, L >> level), [f_ext, c_exts[level - 1]],
                [ext, ext, shape, shapes[level + 1]], [ext, wide_part],
            )
        fields.append(v)
        kept.append((fd, w))

    group = L >> SPLIT
    f_whole, coef_whole = gathered(dims, source[0], coefs[SPLIT][0], 2 * SPLIT)
    scratch = []
    nx, ny = f_whole.shape[0], f_whole.shape[1]
    for level in range(SPLIT, LEVELS - 1):
        scratch.append((1, nx // 2, ny, L))
        nx, ny = nx // 2, ny // 2
    e = call(functools.partial(whole_kernel, SPLIT, group), [f_whole, coef_whole], f_whole.shape, scratch)

    h = W // 2
    e = jnp.concatenate([e[-h:], e, e[:h]], 0)
    e = jnp.concatenate([e[:, -h:], e, e[:, :h]], 1)
    sx, sy = shapes[SPLIT][1], shapes[SPLIT][2]
    e = lax.dynamic_slice(
        e, (lax.axis_index("gx") * sx, lax.axis_index("gy") * sy, 0), (sx + 2 * h, sy + 2 * h, L)
    )
    level = SPLIT - 1
    (t_ext,) = with_halo(dims, [fields[level]], SPLIT + level, True)
    ext = extended(shapes[level])
    t = call(
        functools.partial(up_last_kernel, 0.25**level, L >> level),
        [t_ext, e, *kept[level], fields[level - 1]], shapes[level - 1],
        [ext, (sx + 2 * h, ext[2], L), (shapes[level][1], 2 * shapes[level][2], L)],
    )
    for level in range(SPLIT - 2, 0, -1):
        (t_ext,) = with_halo(dims, [t], SPLIT + level, True)
        ext, shape = extended(shapes[level]), shapes[level]
        t = call(
            functools.partial(up_kernel, 0.25**level, L >> level), [t_ext, *kept[level], fields[level - 1]],
            shapes[level - 1], [ext, (shape[1], 2 * shape[2], L)],
        )
    shape = shapes[0]
    scratch = [pltpu.VMEM(extended(shape), jnp.float32)]
    for _ in range(shape[0]):
        scratch += halo_scratch(1, shape[1], shape[2], True)
    return remote_kernel(
        functools.partial(last_up_kernel, dims), [t, *kept[0]], [shape], scratch, SPLIT
    )[0]


def solution(mesh):
    spec = P(None, "gx", "gy", None)
    dims = (mesh.shape["gx"], mesh.shape["gy"])
    return jax.shard_map(functools.partial(local, dims), mesh=mesh, in_specs=(spec, spec), out_specs=spec, check_vma=False)
```

```python
import functools
import jax
import jax.numpy as jnp
import numpy as np
from jax import lax
from jax.experimental import pallas as pl
from jax.experimental.pallas import tpu as pltpu
from jax.sharding import PartitionSpec as P

LEVELS = 6
SPLIT = 3
W = 4
L = 128
VMEM = pl.BlockSpec(memory_space=pltpu.VMEM)


def iota(shape, dim):
    return lax.broadcasted_iota(jnp.int32, shape, dim)


def z_sum(v, group):
    axis = v.ndim - 1
    if group == L:
        return pltpu.roll(v, 1, axis) + pltpu.roll(v, L - 1, axis)
    place = iota(v.shape, axis) % group
    up = jnp.where(place == group - 1, pltpu.roll(v, group - 1, axis), pltpu.roll(v, L - 1, axis))
    down = jnp.where(place == 0, pltpu.roll(v, L - group + 1, axis), pltpu.roll(v, 1, axis))
    return up + down


def y_sum(v):
    axis, n = v.ndim - 2, v.shape[-2]
    return pltpu.roll(v, 1, axis) + pltpu.roll(v, n - 1, axis)


def squeeze_matrix(half, scale):
    source, target = iota((L, L), 0), iota((L, L), 1)
    return jnp.where(target == source // 2 + half * (L // 2), scale, 0.0).astype(jnp.float32)


def spread_matrix(half):
    source, target = iota((L, L), 0), iota((L, L), 1)
    return jnp.where(source == target // 2 + half * (L // 2), 1.0, 0.0).astype(jnp.float32)


def dot(a, b):
    return jnp.dot(a, b, preferred_element_type=jnp.float32, precision=lax.Precision.HIGHEST)


def fold(part, first, rows):
    count, nx = part.shape[0], part.shape[1]
    outs = []
    for a in range(0, count, 2):
        total = None
        for h in range(min(2, count - a)):
            m = squeeze_matrix(h, 0.125)
            even = jnp.concatenate([part[a + h, x, pl.ds(first, rows, stride=2), :] for x in range(nx)], 0)
            odd = jnp.concatenate([part[a + h, x, pl.ds(first + 1, rows, stride=2), :] for x in range(nx)], 0)
            term = dot(even + odd, m)
            total = term if total is None else total + term
        outs.append(total.reshape(nx, rows, L))
    return outs


def half_sweep(v, f_ref, w_ref, colour, low, high, group, comps=None):
    rows = v.shape[2]
    comps = range(v.shape[0]) if comps is None else comps
    parity = (iota((rows, L), 0) + iota((rows, L), 1)) % 2
    at_once = 4 if len(comps) == 1 else 2

    def some(start, count):
        for k in range(count):
            x = start + k
            mask = parity == (colour + low + k) % 2
            for c in comps:
                mid = v[c, x]
                total = v[c, x - 1] + v[c, x + 1] + y_sum(mid) + z_sum(mid, group)
                v[c, x] = jnp.where(mask, f_ref[c, x] + w_ref[c, x] * total, mid)

    def body(step, carry):
        some(low + at_once * step, at_once)
        return carry

    steps, left = divmod(high - low, at_once)
    lax.fori_loop(0, steps, body, 0)
    if left:
        some(high - left, left)


def down_kernel(scale, group, f_in, c_in, f_out, w_out, v_out, g_out, v, part):
    down(scale, group, range(v.shape[0]), f_in, c_in, f_out, w_out, v_out, v, part)
    for a, g in enumerate(fold(part, W, v_out.shape[2] // 2)):
        g_out[a] = g


def down(scale, group, comps, f_in, c_in, f_out, w_out, v_out, v, part):
    nx, ny = v_out.shape[1], v_out.shape[2]
    ex, rows = f_in.shape[1], f_in.shape[2]
    parity = (iota((rows, L), 0) + iota((rows, L), 1)) % 2

    def first(step, carry):
        for k in range(2):
            x = 2 * step + k
            for c in comps:
                inverse = 1.0 / (c_in[c, x] + 6.0 * scale)
                fd = f_in[c, x] * inverse
                f_out[c, x] = fd
                w_out[c, x] = scale * inverse
                v[c, x] = jnp.where(parity == k, fd, 0.0)
        return carry

    lax.fori_loop(0, ex // 2, first, 0)
    half_sweep(v, f_out, w_out, 1, 1, ex - 1, group, comps)
    half_sweep(v, f_out, w_out, 0, 2, ex - 2, group, comps)
    half_sweep(v, f_out, w_out, 1, 3, ex - 3, group, comps)

    def last(step, carry):
        for c in comps:
            total = None
            for k in range(2):
                x = W + 2 * step + k
                mid = v[c, x]
                nb = v[c, x - 1] + v[c, x + 1] + y_sum(mid) + z_sum(mid, group)
                r = f_in[c, x] - (c_in[c, x] * mid + scale * (6.0 * mid - nb))
                v_out[c, 2 * step + k] = v[c, x, W : W + ny, :]
                total = r if total is None else total + r
            part[c, step] = total
        return carry

    lax.fori_loop(0, nx // 2, last, 0)


def post(v, f_ref, w_ref, group, comps=None):
    ex = v.shape[1]
    for p, colour in ((1, 0), (2, 1), (3, 0), (4, 1)):
        half_sweep(v, f_ref, w_ref, colour, p, ex - p, group, comps)


def up_kernel(scale, group, t_in, f_in, w_in, fine, out, v, t):
    def copy(x, carry):
        for c in range(t_in.shape[0]):
            v[c, x] = t_in[c, x]
        return carry

    lax.fori_loop(0, t_in.shape[1], copy, 0)
    finish(v, f_in, w_in, group, fine, out, t)


def finish(v, f_in, w_in, group, fine, out, t):
    post(v, f_in, w_in, group)
    ex, ey = v.shape[1], v.shape[2]
    nx, ny = ex - 2 * W, ey - 2 * W
    for c in range(v.shape[0]):
        for h in range(2):
            q = dot(v[c, W : W + nx, W : W + ny, :].reshape(nx * ny, L), spread_matrix(h)).reshape(nx, ny, L)
            for x in range(nx):
                t[x, pl.ds(0, ny, stride=2), :] = q[x]
                t[x, pl.ds(1, ny, stride=2), :] = q[x]
            for x in range(nx):
                for k in range(2):
                    out[2 * c + h, 2 * x + k] = fine[2 * c + h, 2 * x + k] + t[x]


def up_last_kernel(scale, group, t_in, e_in, f_in, w_in, fine, out, v, te, t):
    for i in range(e_in.shape[0]):
        q = dot(e_in[i], spread_matrix(0))
        n = q.shape[0]
        te[i, pl.ds(0, n, stride=2), :] = q
        te[i, pl.ds(1, n, stride=2), :] = q
        for k in range(2):
            v[0, 2 * i + k] = t_in[0, 2 * i + k] + te[i]
    finish(v, f_in, w_in, group, fine, out, t)


def whole_neighbours(v, group):
    up = jnp.concatenate([v[1:], v[:1]], 0)
    down = jnp.concatenate([v[-1:], v[:-1]], 0)
    return up + down + y_sum(v) + z_sum(v, group)


def whole_cycle(level, f, coef, group, scratch):
    scale = 0.25**level
    inverse = 1.0 / (coef + 6.0 * scale)
    fd, w = f * inverse, scale * inverse
    parity = (iota(f.shape, 0) + iota(f.shape, 1) + iota(f.shape, 2)) % 2

    def sweep(v, colour):
        return jnp.where(parity == colour, fd + w * whole_neighbours(v, group), v)

    v = jnp.where(parity == 0, fd, 0.0)
    v = sweep(sweep(sweep(v, 1), 0), 1)
    if level == LEVELS - 1:
        return v
    part = scratch[0]
    nx, ny = f.shape[0], f.shape[1]

    def coarse(u):
        pairs = u.reshape(nx // 2, 2, ny, L)
        part[0] = pairs[:, 0] + pairs[:, 1]
        return fold(part, 0, ny // 2)[0]

    g = coarse(f - (coef * v + scale * (6.0 * v - whole_neighbours(v, group))))
    c = coarse(coef)
    e = whole_cycle(level + 1, g, c, group // 2, scratch[1:])
    q = dot(e.reshape(nx // 2 * (ny // 2), L), spread_matrix(0)).reshape(nx // 2, ny // 2, L)
    for x in range(nx // 2):
        part[0, x, pl.ds(0, ny // 2, stride=2), :] = q[x]
        part[0, x, pl.ds(1, ny // 2, stride=2), :] = q[x]
    t = part[0]
    v = v + jnp.concatenate([t[:, None], t[:, None]], 1).reshape(nx, ny, L)
    for colour in (0, 1, 0, 1):
        v = sweep(v, colour)
    return v


def whole_kernel(level, group, f_in, c_in, out, *scratch):
    out[...] = whole_cycle(level, f_in[...], c_in[...], group, scratch)


def coefs_kernel(c_in, *refs):
    outs, parts = refs[: len(refs) // 2], refs[len(refs) // 2 :]
    source = c_in
    for out, part in zip(outs, parts):
        for a in range(part.shape[0]):
            for x in range(part.shape[1]):
                part[a, x] = source[a, 2 * x] + source[a, 2 * x + 1]
        for a, g in enumerate(fold(part, 0, part.shape[2] // 2)):
            out[a] = g
        source = out


def call(kernel, inputs, outs, scratch):
    one = not isinstance(outs, list)
    shapes = [jax.ShapeDtypeStruct(s, jnp.float32) for s in ([outs] if one else outs)]
    result = pl.pallas_call(
        kernel,
        out_shape=shapes,
        in_specs=[VMEM] * len(inputs),
        out_specs=[VMEM] * len(shapes),
        scratch_shapes=[pltpu.VMEM(s, jnp.float32) for s in scratch],
        compiler_params=pltpu.CompilerParams(vmem_limit_bytes=48 * 1024 * 1024),
    )(*inputs)
    return result[0] if one else result


def greet(devices):
    barrier = pltpu.get_barrier_semaphore()
    for device in devices:
        pl.semaphore_signal(barrier, inc=1, device_id=device, device_id_type=pl.DeviceIdType.MESH)
    return barrier, len(devices)


SIDES = [(-1, 0), (1, 0), (0, -1), (0, 1), (-1, -1), (-1, 1), (1, -1), (1, 1)]


def merged(v):
    pairs = v.reshape((v.shape[0] // 2, 2) + v.shape[1:])
    odd = (iota(v.shape[1:], 0) + iota(v.shape[1:], 1)) % 2 == 1
    return jnp.where(odd, pairs[:, 0], pairs[:, 1])


def doubled(m):
    return jnp.concatenate([m[:, None], m[:, None]], 1).reshape((2 * m.shape[0],) + m.shape[1:])


def ring(dims):
    me_x, me_y = lax.axis_index("gx"), lax.axis_index("gy")
    return [
        (lax.rem(me_x + dx + dims[0], dims[0]), lax.rem(me_y + dy + dims[1], dims[1])) for dx, dy in SIDES
    ]


BUFFERS = 7


def halo_scratch(count, nx, ny, merge):
    w, long = (W // 2, nx // 2) if merge else (W, nx)
    flat, tall = (2, count, w, ny, L), (2, count, long, W, L)
    shapes = [flat, tall, flat, tall, (2, 2, count, w, W, L)]
    return [pltpu.VMEM(s, jnp.float32) for s in shapes] + [pltpu.SemaphoreType.DMA((len(SIDES),))] * 2


class Halo:
    def __init__(self, devices, merge, sources, targets, buffers):
        self.merge, self.sources, self.targets = merge, sources, targets
        self.xs, self.ys, self.xr, self.yr, self.cr, send_sem, recv_sem = buffers
        self.nx, self.ny = sources[0][0].shape[1], sources[0][0].shape[2]
        w, long = self.xs.shape[2], self.ys.shape[2]
        self.copies = []
        for k, (dx, dy) in enumerate(SIDES):
            sx, sy = int(dx > 0), int(dy > 0)
            if dy == 0:
                source, target = self.xs.at[sx], self.xr.at[sx]
            elif dx == 0:
                source, target = self.ys.at[sy], self.yr.at[sy]
            else:
                source, target = self.ys.at[sy, :, pl.ds((long - w) * sx, w)], self.cr.at[sx, sy]
            self.copies.append(
                pltpu.make_async_remote_copy(
                    src_ref=source, dst_ref=target, send_sem=send_sem.at[k], recv_sem=recv_sem.at[k],
                    device_id=devices[k], device_id_type=pl.DeviceIdType.MESH,
                )
            )

    def stage(self):
        pack = merged if self.merge else lambda v: v
        nx, ny = self.nx, self.ny
        for at, (ref, c) in enumerate(self.sources):
            self.xs[0, at] = pack(ref[c, 0:W])
            self.xs[1, at] = pack(ref[c, nx - W : nx])
            self.ys[0, at] = pack(ref[c, :, 0:W, :])
            self.ys[1, at] = pack(ref[c, :, ny - W : ny, :])

    def start(self):
        for copy in self.copies:
            copy.start()

    def middle(self):
        for (ref, c), (out, d) in zip(self.sources, self.targets):
            out[d, W : W + self.nx, W : W + self.ny, :] = ref[c]

    def wait(self):
        for copy in self.copies:
            copy.wait()

    def edges(self):
        unpack = doubled if self.merge else lambda v: v
        nx, ny = self.nx, self.ny
        for at, (out, c) in enumerate(self.targets):
            for s in range(2):
                first_x, first_y = (W + nx, W + ny) if s == 0 else (0, 0)
                out[c, first_x : first_x + W, W : W + ny, :] = unpack(self.xr[s, at])
                out[c, W : W + nx, first_y : first_y + W, :] = unpack(self.yr[s, at])
                for u in range(2):
                    corner = W + ny if u == 0 else 0
                    out[c, first_x : first_x + W, corner : corner + W, :] = unpack(self.cr[s, u, at])


def pairs_of(refs):
    return [(ref, c) for ref in refs for c in range(ref.shape[0])]


def halo_kernel(dims, merge, n, *refs):
    devices = ring(dims)
    barrier, count = greet(devices)
    halo = Halo(devices, merge, pairs_of(refs[:n]), pairs_of(refs[n : 2 * n]), refs[2 * n :])
    halo.stage()
    pl.semaphore_wait(barrier, count)
    halo.start()
    halo.middle()
    halo.wait()
    halo.edges()


def in_turn(halos, ahead, work, tail):
    for k in range(ahead):
        if k:
            halos[k].stage()
        halos[k].start()
    for k, halo in enumerate(halos):
        if k + ahead < len(halos):
            halos[k + ahead].stage()
        halo.middle()
        halo.wait()
        if k + ahead < len(halos):
            halos[k + ahead].start()
        if k + 1 == len(halos):
            for other in tail:
                other.start()
        halo.edges()
        work(k)
    for other in tail:
        other.middle()
        other.wait()
        other.edges()


def first_down_kernel(dims, splits, *refs):
    f_in, c_in = refs[:2]
    coarse = refs[2 : 2 + splits]
    f_out, w_out, v_out, g_out = refs[2 + splits : 6 + splits]
    coarse_out = refs[6 + splits : 6 + 2 * splits]
    f_ext, c_ext, v, part = refs[6 + 2 * splits : 10 + 2 * splits]
    rest = refs[10 + 2 * splits :]
    devices = ring(dims)
    barrier, count = greet(devices)
    parts = f_in.shape[0]
    halos = [
        Halo(
            devices, False, [(f_in, c), (c_in, c)], [(f_ext, c), (c_ext, c)],
            rest[BUFFERS * c : BUFFERS * (c + 1)],
        )
        for c in range(parts)
    ]
    tail = [
        Halo(
            devices, False, pairs_of([coarse[i]]), pairs_of([coarse_out[i]]),
            rest[BUFFERS * (parts + i) : BUFFERS * (parts + i + 1)],
        )
        for i in range(splits)
    ]
    halos[0].stage()
    pl.semaphore_wait(barrier, count)
    for other in tail:
        other.stage()

    def work(c):
        down(1.0, L, [c], f_ext, c_ext, f_out, w_out, v_out, v, part)

    in_turn(halos, min(2, parts), work, tail)
    for a, g in enumerate(fold(part, W, v_out.shape[2] // 2)):
        g_out[a] = g


def last_up_kernel(dims, t_in, f_in, w_in, out, v, *rest):
    devices = ring(dims)
    barrier, count = greet(devices)
    parts, nx, ny = out.shape[0], out.shape[1], out.shape[2]
    halos = [
        Halo(devices, True, [(t_in, c)], [(v, c)], rest[BUFFERS * c : BUFFERS * (c + 1)])
        for c in range(parts)
    ]
    halos[0].stage()
    pl.semaphore_wait(barrier, count)

    def work(c):
        post(v, f_in, w_in, L, [c])
        out[c] = v[c, W : W + nx, W : W + ny, :]

    in_turn(halos, parts, work, [])


def remote_kernel(kernel, inputs, outs, scratch, collective_id):
    return pl.pallas_call(
        kernel,
        out_shape=[jax.ShapeDtypeStruct(s, jnp.float32) for s in outs],
        in_specs=[VMEM] * len(inputs),
        out_specs=[VMEM] * len(outs),
        scratch_shapes=scratch,
        compiler_params=pltpu.CompilerParams(
            vmem_limit_bytes=48 * 1024 * 1024, collective_id=collective_id, has_side_effects=True
        ),
    )(*inputs)


def with_halo(dims, arrays, collective_id, merge=False):
    count = sum(a.shape[0] for a in arrays)
    nx, ny = arrays[0].shape[1], arrays[0].shape[2]
    return remote_kernel(
        functools.partial(halo_kernel, dims, merge, len(arrays)), arrays,
        [(a.shape[0], nx + 2 * W, ny + 2 * W, L) for a in arrays],
        halo_scratch(count, nx, ny, merge), collective_id,
    )


def gather_kernel(dims, f_in, c_in, t_in, f_out, c_out, t_out, slots, send_sem, recv_sem, *buffers):
    me_x, me_y = lax.axis_index("gx"), lax.axis_index("gy")
    along_x = [(lax.rem(me_x + d, dims[0]), me_y) for d in range(1, dims[0])]
    along_y = [(me_x, lax.rem(me_y + d, dims[1])) for d in range(1, dims[1])]
    devices = ring(dims)
    barrier, count = greet(along_x + along_y + devices[4:])
    halo = Halo(devices, True, pairs_of([t_in]), pairs_of([t_out]), buffers)
    halo.stage()
    half = iota(f_in.shape, 2) < L // 2
    slots[me_y, me_x] = jnp.where(half, f_in[...], pltpu.roll(c_in[...], L // 2, 2))
    pl.semaphore_wait(barrier, count)
    at = 0
    for others, part in ((along_x, slots.at[me_y, me_x]), (along_y, slots.at[me_y])):
        copies = []
        for device in others:
            copies.append(
                pltpu.make_async_remote_copy(
                    src_ref=part, dst_ref=part, send_sem=send_sem.at[at], recv_sem=recv_sem.at[at],
                    device_id=device, device_id_type=pl.DeviceIdType.MESH,
                )
            )
            at += 1
        for copy in copies:
            copy.start()
        if others is along_x:
            halo.middle()
        for copy in copies:
            copy.wait()
        if others is along_x:
            halo.start()
    rows, ny = f_out.shape[0], f_in.shape[1]
    for j in range(dims[1]):
        part = slots[j].reshape(rows, ny, L)
        low = iota(part.shape, 2) < L // 2
        f_out[:, j * ny : (j + 1) * ny, :] = jnp.where(low, part, 0.0)
        c_out[:, j * ny : (j + 1) * ny, :] = jnp.where(low, pltpu.roll(part, L // 2, 2), 0.0)
    halo.wait()
    halo.edges()


def gathered(dims, f, coef, t, collective_id):
    shape = (f.shape[0] * dims[0], f.shape[1] * dims[1], L)
    copies = dims[0] + dims[1] - 2
    return remote_kernel(
        functools.partial(gather_kernel, dims), [f, coef, t],
        [shape, shape, (t.shape[0], t.shape[1] + 2 * W, t.shape[2] + 2 * W, L)],
        [pltpu.VMEM((dims[1], dims[0]) + f.shape, jnp.float32)]
        + [pltpu.SemaphoreType.DMA((copies,))] * 2
        + halo_scratch(t.shape[0], t.shape[1], t.shape[2], True),
        collective_id,
    )


def local(dims, rhs, coefficient):
    shapes = [rhs.shape]
    for _ in range(SPLIT):
        k, a, b, c = shapes[-1]
        shapes.append(((k + 1) // 2, a // 2, b // 2, L))

    def extended(shape):
        return (shape[0], shape[1] + 2 * W, shape[2] + 2 * W, L)

    coarser = call(
        coefs_kernel, [coefficient], shapes[1:],
        [(s[0], s[1] // 2, s[2], L) for s in shapes[:-1]],
    )
    coefs = [coefficient] + list(coarser)

    source = rhs
    fields, kept = [], []
    for level in range(SPLIT):
        shape = shapes[level]
        ext = extended(shape)
        wide_part = (shape[0], shape[1] // 2, ext[2], L)
        if level == 0:
            scratch = [pltpu.VMEM(x, jnp.float32) for x in (ext, ext, ext, wide_part)]
            for _ in range(shape[0]):
                scratch += halo_scratch(2, shape[1], shape[2], False)
            for x in shapes[1:SPLIT]:
                scratch += halo_scratch(x[0], x[1], x[2], False)
            fd, w, v, source, *c_exts = remote_kernel(
                functools.partial(first_down_kernel, dims, SPLIT - 1), [source] + coefs[:SPLIT],
                [ext, ext, shape, shapes[1]] + [extended(x) for x in shapes[1:SPLIT]], scratch, 0,
            )
        else:
            (f_ext,) = with_halo(dims, [source], level)
            fd, w, v, source = call(
                functools.partial(down_kernel, 0.25**level, L >> level), [f_ext, c_exts[level - 1]],
                [ext, ext, shape, shapes[level + 1]], [ext, wide_part],
            )
        fields.append(v)
        kept.append((fd, w))

    group = L >> SPLIT
    f_whole, coef_whole, t_ext = gathered(dims, source[0], coefs[SPLIT][0], fields[-1], 2 * SPLIT)
    scratch = []
    nx, ny = f_whole.shape[0], f_whole.shape[1]
    for level in range(SPLIT, LEVELS - 1):
        scratch.append((1, nx // 2, ny, L))
        nx, ny = nx // 2, ny // 2
    e = call(functools.partial(whole_kernel, SPLIT, group), [f_whole, coef_whole], f_whole.shape, scratch)

    h = W // 2
    e = jnp.concatenate([e[-h:], e, e[:h]], 0)
    e = jnp.concatenate([e[:, -h:], e, e[:, :h]], 1)
    sx, sy = shapes[SPLIT][1], shapes[SPLIT][2]
    e = lax.dynamic_slice(
        e, (lax.axis_index("gx") * sx, lax.axis_index("gy") * sy, 0), (sx + 2 * h, sy + 2 * h, L)
    )
    level = SPLIT - 1
    ext = extended(shapes[level])
    t = call(
        functools.partial(up_last_kernel, 0.25**level, L >> level),
        [t_ext, e, *kept[level], fields[level - 1]], shapes[level - 1],
        [ext, (sx + 2 * h, ext[2], L), (shapes[level][1], 2 * shapes[level][2], L)],
    )
    for level in range(SPLIT - 2, 0, -1):
        (t_ext,) = with_halo(dims, [t], SPLIT + level, True)
        ext, shape = extended(shapes[level]), shapes[level]
        t = call(
            functools.partial(up_kernel, 0.25**level, L >> level), [t_ext, *kept[level], fields[level - 1]],
            shapes[level - 1], [ext, (shape[1], 2 * shape[2], L)],
        )
    shape = shapes[0]
    scratch = [pltpu.VMEM(extended(shape), jnp.float32)]
    for _ in range(shape[0]):
        scratch += halo_scratch(1, shape[1], shape[2], True)
    return remote_kernel(
        functools.partial(last_up_kernel, dims), [t, *kept[0]], [shape], scratch, SPLIT
    )[0]


def solution(mesh):
    spec = P(None, "gx", "gy", None)
    dims = (mesh.shape["gx"], mesh.shape["gy"])
    return jax.shard_map(functools.partial(local, dims), mesh=mesh, in_specs=(spec, spec), out_specs=spec, check_vma=False)
```
